32 devices in a mesh: comp: 4 (over y, x), site: 8 (over z, core).
Axes of the slice: x: 2, y: 2, z: 4, core: 2. Of those that a mesh axis runs over, the one named last changes fastest.
Arguments:
- factors: bfloat16 [24, 1024, 6144], P('comp', None, 'site'), may hold values from -0.1875 to 0.1875
- normals: bfloat16 [24, 32, 1024], P('comp', 'site'), may hold values from -6 to 6
- loadings: float32 [24, 24], replicated, may hold values from -1.25 to 1.25
- mean_ln: float32 [24, 6144], P(None, 'site'), may hold values from -4 to -0.5
- sigma: float32 [24, 6144], P(None, 'site'), may hold values from 0.3 to 1
Outputs:
- ln_motion: bfloat16 [32, 24, 6144], P(('comp', 'site'))
The draws below stay inside these ranges and needn't reach their ends.
All inputs are finite; a program needn't handle non-finite values.
Results may differ from the reference program's by a relative error of at most 0.006.
Values may be sent and summed in bfloat16 or wider, within the bound.
A program may use at most 128 MiB of HBM per device.

```python
import jax
import jax.numpy as jnp
from jax import lax

PERIODS = 24
RANK = 1024
S_DEV = 768
COMPS = 24
SITES = 6144
REAL = 32


def block_scale(stream_key, shape, shards, least, high):
    def one(position, parts):
        heights = jax.random.uniform(jax.random.fold_in(jax.random.fold_in(stream_key, 6), position), (parts,), jnp.float32, least / len(shards), high / len(shards))
        return jnp.repeat(jnp.exp(heights), shape[position] // parts).reshape((-1,) + (1,) * (len(shape) - position - 1))

    loudness = one(*shards[0])
    for cut in shards[1:]:
        loudness = loudness * one(*cut)
    return loudness


def centred(stream_key, dims, deviation, bound, shards=(), held_as=jnp.bfloat16):
    result = jax.random.normal(stream_key, dims, jnp.float32) * deviation
    if len(shards) > 0:
        result = block_scale(stream_key, dims, shards, -0.22, 0.18) * result
    return jnp.clip(result, min=-bound, max=bound).astype(held_as)


def setup_inputs(seed: int = 0) -> dict:
    splits = jax.random.split(jax.random.key(seed), 6)
    return {
        "factors": centred(splits[0], (COMPS, RANK, SITES), RANK ** -0.5, 0.1875, ((0, 4), (2, 8))),
        "normals": centred(splits[1], (COMPS, REAL, RANK), 1.0, 6.0, ((0, 4), (1, 8))),
        "loadings": centred(splits[2], (PERIODS, COMPS), COMPS ** -0.5, 1.25, (), jnp.float32),
        "mean_ln": jnp.clip(-4.0 + 3.5 * jax.random.uniform(splits[3], (PERIODS, SITES), jnp.float32) ** block_scale(splits[3], (PERIODS, SITES), ((1, 8),), -0.2, 0.2), -4.0, -0.5),
        "sigma": jnp.clip(0.3 + 0.7 * jax.random.uniform(splits[4], (PERIODS, SITES), jnp.float32) ** block_scale(splits[4], (PERIODS, SITES), ((1, 8),), -0.2, 0.2), 0.3, 1.0),
    }


def reference(factors, normals, loadings, mean_ln, sigma):
    blocks = SITES // S_DEV
    draws_f = normals.astype(jnp.float32)

    def one_block(index):
        start = (index * S_DEV).astype(jnp.int32)
        piece = lax.dynamic_slice_in_dim(factors, start, S_DEV, 2).astype(jnp.float32)
        fields = jnp.einsum("krj,kjs->krs", draws_f, piece).astype(jnp.bfloat16)
        eps = jnp.einsum("pk,krs->rps", loadings, fields.astype(jnp.float32), precision=lax.Precision.HIGHEST)
        mean_part = lax.dynamic_slice_in_dim(mean_ln, start, S_DEV, 1)
        sigma_part = lax.dynamic_slice_in_dim(sigma, start, S_DEV, 1)
        return (mean_part[None] + sigma_part[None] * eps).astype(jnp.bfloat16)

    stacked = lax.map(one_block, jnp.arange(blocks, dtype=jnp.int32))
    return jnp.transpose(stacked, (1, 2, 0, 3)).reshape(REAL, PERIODS, SITES)
```

```python
import functools

import jax
import jax.numpy as jnp
from jax import lax
from jax.experimental import pallas as pl
from jax.experimental.pallas import tpu as pltpu
from jax.sharding import PartitionSpec as P

MESH = pl.DeviceIdType.MESH
QUARTERS = 4
LANES = 256


def each(start, stop, step):
    if stop - start <= 8:
        for i in range(start, stop):
            step(i)
    else:
        lax.fori_loop(start, stop, lambda i, carry: (step(i), carry)[1], 0)


def kernel(
    n_comp, n_site,
    factors, normals_h, loadings_h, mean_ln, sigma, got_m,
    weights, normals, loadings, drawn, mean_v, sigma_v, mix, sent_f, got_f, sent_m,
    w_sem, in_sem, d_send, d_pass, d_recv, f_send, f_recv, m_send, m_recv, keep_sem,
):
    me_c, me_s = lax.axis_index("comp"), lax.axis_index("site")
    ks, rows, rank = normals.shape
    periods, comps = loadings.shape
    s_dev = factors.shape[2]
    chunks = s_dev // LANES
    groups = n_site // 2 // n_comp
    chips = n_site // 2
    deep = rank // QUARTERS
    f32, bf16 = jnp.float32, jnp.bfloat16

    def load_w(t, k):
        lanes = pl.ds(t * LANES, LANES)
        return pltpu.make_async_copy(
            factors.at[k, :, lanes], weights.at[t, k], w_sem.at[t, k]
        )

    mean_copy = pltpu.make_async_copy(mean_ln, mean_v, in_sem.at[0])
    sigma_copy = pltpu.make_async_copy(sigma, sigma_v, in_sem.at[1])
    normals_copy = pltpu.make_async_copy(normals_h, normals, in_sem.at[2])
    loadings_copy = pltpu.make_async_copy(loadings_h, loadings, in_sem.at[3])
    normals_copy.start()

    barrier = pltpu.get_barrier_semaphore()

    def greet_s(d):
        pl.semaphore_signal(
            barrier, inc=1, device_id={"site": me_s ^ d}, device_id_type=MESH
        )

    def greet_c(d):
        pl.semaphore_signal(
            barrier, inc=1, device_id={"comp": me_c ^ d}, device_id_type=MESH
        )

    each(1, n_site, lambda d: greet_s(n_site - d))
    each(1, n_comp, lambda d: greet_c(n_comp - d))

    loadings_copy.start()
    for t in range(chunks):
        for k in range(ks):
            load_w(t, k).start()
    mean_copy.start()
    sigma_copy.start()
    normals_copy.wait()

    for k in range(ks):
        x = normals[k].astype(f32)
        x = jnp.concatenate([x[:, q * deep:(q + 1) * deep] for q in range(QUARTERS)], axis=0)
        drawn[me_s, 16 * k:16 * (k + 1), :] = x.astype(bf16)

    pl.semaphore_wait(barrier, n_site - 1 + n_comp - 1)

    pairs = ks // 2

    def draws(slot, send_sem, peer):
        return pltpu.make_async_remote_copy(
            src_ref=drawn.at[slot], dst_ref=drawn.at[slot],
            send_sem=send_sem, recv_sem=d_recv.at[slot],
            device_id={"site": peer}, device_id_type=MESH,
        )

    def across(d):
        return draws(me_s, d_send.at[d], me_s ^ (2 * d))

    def beside(d):
        return draws(me_s ^ (2 * d), d_pass.at[d], me_s ^ 1)

    def from_beside(d):
        return draws(me_s ^ (2 * d) ^ 1, d_pass.at[d], me_s ^ 1)

    each(1, chips, lambda d: across(chips - d).start())
    beside(0).start()

    spread = (
        lax.broadcasted_iota(jnp.int32, (comps, comps * 8), 1) >> 3
        == lax.broadcasted_iota(jnp.int32, (comps, comps * 8), 0)
    ).astype(f32).astype(bf16)
    turn = lax.broadcasted_iota(jnp.int32, (periods, comps * 8), 1) & 7
    loadings_copy.wait()
    rest = loadings[...]
    for i in range(3):
        term = rest.astype(bf16)
        rest = rest - term.astype(f32)
        wide = jnp.dot(term, spread, preferred_element_type=f32)
        full = jnp.concatenate([jnp.where(turn == r, wide, 0.0) for r in range(8)], axis=0)
        mix[i * periods * 8:(i + 1) * periods * 8, :] = full.astype(bf16)

    def pass_on(d):
        beside(d).wait_recv()
        beside(d).start()

    quarter = (lax.broadcasted_iota(jnp.int32, (n_site * 16, deep), 0) >> 2) & 3
    low = lax.broadcasted_iota(jnp.int32, (chips, 8, LANES), 1) < 4

    def product(t, k):
        x = drawn[:, 16 * k:16 * (k + 1), :].reshape(n_site * 16, deep).astype(f32)
        lhs = jnp.concatenate(
            [jnp.where(quarter == q, x, 0.0).astype(bf16) for q in range(QUARTERS)], axis=1
        )
        y = jnp.dot(lhs, weights[t, k], preferred_element_type=f32)
        y = y.reshape(n_site, 2, 8, LANES)
        y = y[:, 0] + y[:, 1]
        y = y + pltpu.roll(y, 4, 1)
        y = y.reshape(chips, 2, 8, LANES)
        return jnp.where(low, y[:, 0], y[:, 1])

    def f_copy(t, d):
        peer = me_c ^ d
        at = pl.ds(pl.multiple_of(me_c * ks * 8, 16), ks * 8)
        return pltpu.make_async_remote_copy(
            src_ref=sent_f.at[t, peer], dst_ref=got_f.at[t, :, at, :],
            send_sem=f_send.at[t, d], recv_sem=f_recv.at[t, d],
            device_id={"comp": peer}, device_id_type=MESH,
        )

    def fields(j, t):
        load_w(t, 2 * j).wait()
        load_w(t, 2 * j + 1).wait()
        both = jnp.concatenate([product(t, 2 * j), product(t, 2 * j + 1)], axis=1).astype(bf16)
        sent_f[t, :, :, 16 * j:16 * (j + 1), :] = both.reshape(n_comp, groups, 16, LANES)

    def send_fields(t):
        for d in range(1, n_comp):
            f_copy(t, n_comp - d).start()
        at = pl.ds(pl.multiple_of(me_c * ks * 8, 16), ks * 8)
        got_f[t, :, at, :] = sent_f[t, me_c]

    def m_copy(t, d):
        peer = me_s ^ d
        return pltpu.make_async_remote_copy(
            src_ref=sent_m.at[t, peer], dst_ref=got_m.at[t, me_s],
            send_sem=m_send.at[t, d], recv_sem=m_recv.at[t, d],
            device_id={"site": peer}, device_id_type=MESH,
        )

    def motions(t):
        for d in range(1, n_comp):
            f_copy(t, d).wait_recv()
        mean = mean_v[:, t * LANES:(t + 1) * LANES]
        dev = sigma_v[:, t * LANES:(t + 1) * LANES]
        n = periods * 8

        def one(g):
            e = jnp.dot(mix[...], got_f[t, g], preferred_element_type=f32)
            e = (e[2 * n:] + e[n:2 * n]) + e[:n]
            m = mean[None] + dev[None] * e.reshape(8, periods, LANES)
            m = jnp.concatenate([m[:, :, :LANES // 2], m[:, :, LANES // 2:]], axis=1)
            sent_m[t, pl.ds(8 * g, 8)] = m.astype(bf16)

        each(0, groups, one)
        each(1, n_site, lambda d: m_copy(t, n_site - d).start())
        m_keep(t).start()

    def m_keep(t):
        return pltpu.make_async_copy(sent_m.at[t, me_s], got_m.at[t, me_s], keep_sem.at[t])

    each(1, chips, pass_on)
    each(0, chips, lambda d: from_beside(d).wait_recv())
    for t in range(chunks):
        for j in range(pairs):
            fields(j, t)
        send_fields(t)
    mean_copy.wait()
    sigma_copy.wait()
    for t in range(chunks):
        motions(t)

    for t in range(chunks):
        each(1, n_site, lambda d: m_copy(t, d).wait_recv())
        m_keep(t).wait()

    each(1, chips, lambda d: across(d).wait_send())
    each(0, chips, lambda d: beside(d).wait_send())
    for t in range(chunks):
        for d in range(1, n_comp):
            f_copy(t, d).wait_send()
        each(1, n_site, lambda d: m_copy(t, d).wait_send())


def arrange(blocks, out):
    chunks, slabs, rows, half = blocks.shape
    periods = rows // 2

    def one(s):
        for t in range(chunks):
            x = blocks[t, s].astype(jnp.float32)
            for h in range(2):
                at = pl.multiple_of((s * chunks + t) * 2 * half + h * half, half)
                out[0, :, pl.ds(at, half)] = x[h * periods:(h + 1) * periods].astype(out.dtype)

    each(0, slabs, one)


def body(n_comp, n_site, factors, normals, loadings, mean_ln, sigma):
    ks, rank, s_dev = factors.shape
    rows = normals.shape[1]
    periods, comps = loadings.shape
    groups = n_site // 2 // n_comp
    chunks = s_dev // LANES
    assert rows == 4 and n_comp == rows and n_site % (2 * n_comp) == 0
    assert n_site & (n_site - 1) == 0
    assert ks % 2 == 0 and periods % 8 == 0 and s_dev % LANES == 0
    bf16 = jnp.bfloat16
    dma = pltpu.SemaphoreType.DMA
    any_ = pl.BlockSpec(memory_space=pl.ANY)
    blocks = pl.pallas_call(
        functools.partial(kernel, n_comp, n_site),
        out_shape=pltpu.VMEM((chunks, n_site, 2 * periods, LANES // 2), bf16),
        in_specs=[any_] * 5,
        out_specs=any_,
        scratch_shapes=[
            pltpu.VMEM((chunks, ks, rank, LANES), bf16),
            pltpu.VMEM(normals.shape, bf16),
            pltpu.VMEM(loadings.shape, jnp.float32),
            pltpu.VMEM((n_site, ks * 16, rank // QUARTERS), bf16),
            pltpu.VMEM((periods, s_dev), jnp.float32),
            pltpu.VMEM((periods, s_dev), jnp.float32),
            pltpu.VMEM((3 * periods * 8, comps * 8), bf16),
            pltpu.VMEM((chunks, n_comp, groups, ks * 8, LANES), bf16),
            pltpu.VMEM((chunks, groups, comps * 8, LANES), bf16),
            pltpu.VMEM((chunks, n_site, 2 * periods, LANES // 2), bf16),
            dma((chunks, ks)), dma((4,)),
            dma((n_site // 2,)), dma((n_site // 2,)), dma((n_site,)),
            dma((chunks, n_comp)), dma((chunks, n_comp)),
            dma((chunks, n_site)), dma((chunks, n_site)), dma((chunks,)),
        ],
        compiler_params=pltpu.CompilerParams(
            collective_id=0, has_side_effects=True, vmem_limit_bytes=40 * 1024 * 1024
        ),
        cost_estimate=pl.CostEstimate(
            flops=2 * ks * rows * n_site * rank * s_dev,
            bytes_accessed=2 * ks * rank * s_dev, transcendentals=0,
        ),
    )(*(pltpu.with_memory_space_constraint(x, pltpu.HBM) for x in (factors, normals, loadings, mean_ln, sigma)))
    return pl.pallas_call(
        arrange,
        out_shape=jax.ShapeDtypeStruct((1, periods, n_site * s_dev), bf16),
        in_specs=[pl.BlockSpec(memory_space=pltpu.VMEM)],
        out_specs=pl.BlockSpec(memory_space=pltpu.VMEM),
        compiler_params=pltpu.CompilerParams(vmem_limit_bytes=40 * 1024 * 1024),
    )(pltpu.with_memory_space_constraint(blocks, pltpu.VMEM))


def solution(mesh):
    in_specs = (
        P("comp", None, "site"),
        P("comp", "site", None),
        P(),
        P(None, "site"),
        P(None, "site"),
    )
    out_specs = P(("comp", "site"), None, None)
    run = functools.partial(body, mesh.shape["comp"], mesh.shape["site"])
    return jax.shard_map(run, mesh=mesh, in_specs=in_specs, out_specs=out_specs, check_vma=False)
```

```python
import functools

import jax
import jax.numpy as jnp
from jax import lax
from jax.experimental import pallas as pl
from jax.experimental.pallas import tpu as pltpu
from jax.sharding import PartitionSpec as P

MESH = pl.DeviceIdType.MESH
QUARTERS = 4
LANES = 256
DRAWS = (235, 85, 190)
MOTIONS = (239, 154, 117)


def each(start, stop, step):
    if stop - start <= 8:
        for i in range(start, stop):
            step(i)
    else:
        lax.fori_loop(start, stop, lambda i, carry: (step(i), carry)[1], 0)


def kernel(
    n_comp, n_site,
    factors, normals_h, loadings_h, mean_ln, sigma, got_m,
    weights, normals, loadings, drawn, mean_v, sigma_v, mix, sent_f, got_f, sent_m,
    w_sem, in_sem, d_send, d_pass, d_recv, f_send, f_recv, m_send, m_recv, keep_sem,
):
    me_c, me_s = lax.axis_index("comp"), lax.axis_index("site")
    ks, rows, rank = normals.shape
    periods, comps = loadings.shape
    s_dev = factors.shape[2]
    chunks = s_dev // LANES
    groups = n_site // 2 // n_comp
    chips = n_site // 2
    deep = rank // QUARTERS
    f32, bf16 = jnp.float32, jnp.bfloat16

    def load_w(t, k):
        lanes = pl.ds(t * LANES, LANES)
        return pltpu.make_async_copy(
            factors.at[k, :, lanes], weights.at[t, k], w_sem.at[t, k]
        )

    mean_copy = pltpu.make_async_copy(mean_ln, mean_v, in_sem.at[0])
    sigma_copy = pltpu.make_async_copy(sigma, sigma_v, in_sem.at[1])
    normals_copy = pltpu.make_async_copy(normals_h, normals, in_sem.at[2])
    loadings_copy = pltpu.make_async_copy(loadings_h, loadings, in_sem.at[3])
    normals_copy.start()

    barrier = pltpu.get_barrier_semaphore()

    def greet_s(d):
        pl.semaphore_signal(
            barrier, inc=1, device_id={"site": me_s ^ d}, device_id_type=MESH
        )

    def greet_c(d):
        pl.semaphore_signal(
            barrier, inc=1, device_id={"comp": me_c ^ d}, device_id_type=MESH
        )

    each(1, n_site, lambda d: greet_s(n_site - d))
    each(1, n_comp, lambda d: greet_c(n_comp - d))

    loadings_copy.start()
    for t in range(chunks):
        for k in range(ks):
            load_w(t, k).start()
    mean_copy.start()
    sigma_copy.start()
    normals_copy.wait()

    for k in range(ks):
        x = normals[k].astype(f32)
        x = jnp.concatenate([x[:, q * deep:(q + 1) * deep] for q in range(QUARTERS)], axis=0)
        drawn[me_s, 16 * k:16 * (k + 1), :] = x.astype(bf16)

    pl.semaphore_wait(barrier, n_site - 1 + n_comp - 1)

    pairs = ks // 2

    def draws(slot, send_sem, peer):
        return pltpu.make_async_remote_copy(
            src_ref=drawn.at[slot], dst_ref=drawn.at[slot],
            send_sem=send_sem, recv_sem=d_recv.at[slot],
            device_id={"site": peer}, device_id_type=MESH,
        )

    def across(d):
        return draws(me_s, d_send.at[d], me_s ^ (2 * d))

    def beside(d):
        return draws(me_s ^ (2 * d), d_pass.at[d], me_s ^ 1)

    def from_beside(d):
        return draws(me_s ^ (2 * d) ^ 1, d_pass.at[d], me_s ^ 1)

    def pick(table):
        return table // lax.shift_left(1, me_s // 2 * 2) % 4

    if chips == 4:
        first, second, last = (pick(table) for table in DRAWS)
        across(first).start()
        across(second).start()
    else:
        each(1, chips, lambda d: across(chips - d).start())
    beside(0).start()

    spread = (
        lax.broadcasted_iota(jnp.int32, (comps, comps * 8), 1) >> 3
        == lax.broadcasted_iota(jnp.int32, (comps, comps * 8), 0)
    ).astype(f32).astype(bf16)
    turn = lax.broadcasted_iota(jnp.int32, (periods, comps * 8), 1) & 7
    loadings_copy.wait()
    rest = loadings[...]
    for i in range(3):
        term = rest.astype(bf16)
        rest = rest - term.astype(f32)
        wide = jnp.dot(term, spread, preferred_element_type=f32)
        full = jnp.concatenate([jnp.where(turn == r, wide, 0.0) for r in range(8)], axis=0)
        mix[i * periods * 8:(i + 1) * periods * 8, :] = full.astype(bf16)

    def pass_on(d):
        beside(d).wait_recv()
        beside(d).start()

    quarter = (lax.broadcasted_iota(jnp.int32, (n_site * 16, deep), 0) >> 2) & 3
    low = lax.broadcasted_iota(jnp.int32, (chips, 8, LANES), 1) < 4

    def product(t, k):
        x = drawn[:, 16 * k:16 * (k + 1), :].reshape(n_site * 16, deep).astype(f32)
        lhs = jnp.concatenate(
            [jnp.where(quarter == q, x, 0.0).astype(bf16) for q in range(QUARTERS)], axis=1
        )
        y = jnp.dot(lhs, weights[t, k], preferred_element_type=f32)
        y = y.reshape(n_site, 2, 8, LANES)
        y = y[:, 0] + y[:, 1]
        y = y + pltpu.roll(y, 4, 1)
        y = y.reshape(chips, 2, 8, LANES)
        return jnp.where(low, y[:, 0], y[:, 1])

    def f_copy(t, d):
        peer = me_c ^ d
        at = pl.ds(pl.multiple_of(me_c * ks * 8, 16), ks * 8)
        return pltpu.make_async_remote_copy(
            src_ref=sent_f.at[t, peer], dst_ref=got_f.at[t, :, at, :],
            send_sem=f_send.at[t, d], recv_sem=f_recv.at[t, d],
            device_id={"comp": peer}, device_id_type=MESH,
        )

    def fields(j, t):
        both = jnp.concatenate([product(t, 2 * j), product(t, 2 * j + 1)], axis=1).astype(bf16)
        sent_f[t, :, :, 16 * j:16 * (j + 1), :] = both.reshape(n_comp, groups, 16, LANES)

    def send_fields(t):
        for d in range(1, n_comp):
            f_copy(t, n_comp - d).start()
        at = pl.ds(pl.multiple_of(me_c * ks * 8, 16), ks * 8)
        got_f[t, :, at, :] = sent_f[t, me_c]

    def m_copy(t, d):
        peer = me_s ^ d
        return pltpu.make_async_remote_copy(
            src_ref=sent_m.at[t, peer], dst_ref=got_m.at[t, me_s],
            send_sem=m_send.at[t, d], recv_sem=m_recv.at[t, d],
            device_id={"site": peer}, device_id_type=MESH,
        )

    def motions(t):
        for d in range(1, n_comp):
            f_copy(t, d).wait_recv()
        mean = mean_v[:, t * LANES:(t + 1) * LANES]
        dev = sigma_v[:, t * LANES:(t + 1) * LANES]
        n = periods * 8

        def one(g):
            e = jnp.dot(mix[...], got_f[t, g], preferred_element_type=f32)
            e = (e[2 * n:] + e[n:2 * n]) + e[:n]
            m = mean[None] + dev[None] * e.reshape(8, periods, LANES)
            m = jnp.concatenate([m[:, :, :LANES // 2], m[:, :, LANES // 2:]], axis=1)
            sent_m[t, pl.ds(8 * g, 8)] = m.astype(bf16)

        each(0, groups, one)
        if chips == 4:
            for table in MOTIONS:
                d = pick(table) * 2
                m_copy(t, d + 1).start()
                m_copy(t, d).start()
            m_copy(t, 1).start()
        else:
            each(1, n_site, lambda d: m_copy(t, n_site - d).start())
        m_keep(t).start()

    def m_keep(t):
        return pltpu.make_async_copy(sent_m.at[t, me_s], got_m.at[t, me_s], keep_sem.at[t])

    if chips == 4:
        across(first).wait_send()
        across(last).start()
    for t in range(chunks):
        for k in range(ks):
            load_w(t, k).wait()
    each(1, chips, pass_on)
    each(0, chips, lambda d: from_beside(d).wait_recv())
    for t in range(chunks):
        for j in range(pairs):
            fields(j, t)
        send_fields(t)
    mean_copy.wait()
    sigma_copy.wait()
    for t in range(chunks):
        motions(t)

    if chips == 4:
        across(second).wait_send()
        across(last).wait_send()
    else:
        each(1, chips, lambda d: across(d).wait_send())
    each(0, chips, lambda d: beside(d).wait_send())
    for t in range(chunks):
        for d in range(1, n_comp):
            f_copy(t, d).wait_send()
    for t in range(chunks):
        m_keep(t).wait()
        each(1, n_site, lambda d: m_copy(t, d).wait_send())
    for t in range(chunks):
        each(1, n_site, lambda d: m_copy(t, d).wait_recv())


def arrange(blocks, out):
    chunks, slabs, rows, half = blocks.shape
    periods = rows // 2

    def one(s):
        for t in range(chunks):
            x = blocks[t, s].astype(jnp.float32)
            for h in range(2):
                at = pl.multiple_of((s * chunks + t) * 2 * half + h * half, half)
                out[0, :, pl.ds(at, half)] = x[h * periods:(h + 1) * periods].astype(out.dtype)

    each(0, slabs, one)


def body(n_comp, n_site, factors, normals, loadings, mean_ln, sigma):
    ks, rank, s_dev = factors.shape
    rows = normals.shape[1]
    periods, comps = loadings.shape
    groups = n_site // 2 // n_comp
    chunks = s_dev // LANES
    assert rows == 4 and n_comp == rows and n_site % (2 * n_comp) == 0
    assert n_site & (n_site - 1) == 0
    assert ks % 2 == 0 and periods % 8 == 0 and s_dev % LANES == 0
    bf16 = jnp.bfloat16
    dma = pltpu.SemaphoreType.DMA
    any_ = pl.BlockSpec(memory_space=pl.ANY)
    blocks = pl.pallas_call(
        functools.partial(kernel, n_comp, n_site),
        out_shape=pltpu.VMEM((chunks, n_site, 2 * periods, LANES // 2), bf16),
        in_specs=[any_] * 5,
        out_specs=any_,
        scratch_shapes=[
            pltpu.VMEM((chunks, ks, rank, LANES), bf16),
            pltpu.VMEM(normals.shape, bf16),
            pltpu.VMEM(loadings.shape, jnp.float32),
            pltpu.VMEM((n_site, ks * 16, rank // QUARTERS), bf16),
            pltpu.VMEM((periods, s_dev), jnp.float32),
            pltpu.VMEM((periods, s_dev), jnp.float32),
            pltpu.VMEM((3 * periods * 8, comps * 8), bf16),
            pltpu.VMEM((chunks, n_comp, groups, ks * 8, LANES), bf16),
            pltpu.VMEM((chunks, groups, comps * 8, LANES), bf16),
            pltpu.VMEM((chunks, n_site, 2 * periods, LANES // 2), bf16),
            dma((chunks, ks)), dma((4,)),
            dma((n_site // 2,)), dma((n_site // 2,)), dma((n_site,)),
            dma((chunks, n_comp)), dma((chunks, n_comp)),
            dma((chunks, n_site)), dma((chunks, n_site)), dma((chunks,)),
        ],
        compiler_params=pltpu.CompilerParams(
            collective_id=0, has_side_effects=True, vmem_limit_bytes=40 * 1024 * 1024
        ),
        cost_estimate=pl.CostEstimate(
            flops=2 * ks * rows * n_site * rank * s_dev,
            bytes_accessed=2 * ks * rank * s_dev, transcendentals=0,
        ),
    )(*(pltpu.with_memory_space_constraint(x, pltpu.HBM) for x in (factors, normals, loadings, mean_ln, sigma)))
    return pl.pallas_call(
        arrange,
        out_shape=jax.ShapeDtypeStruct((1, periods, n_site * s_dev), bf16),
        in_specs=[pl.BlockSpec(memory_space=pltpu.VMEM)],
        out_specs=pl.BlockSpec(memory_space=pltpu.VMEM),
        compiler_params=pltpu.CompilerParams(vmem_limit_bytes=40 * 1024 * 1024),
    )(pltpu.with_memory_space_constraint(blocks, pltpu.VMEM))


def solution(mesh):
    in_specs = (
        P("comp", None, "site"),
        P("comp", "site", None),
        P(),
        P(None, "site"),
        P(None, "site"),
    )
    out_specs = P(("comp", "site"), None, None)
    run = functools.partial(body, mesh.shape["comp"], mesh.shape["site"])
    return jax.shard_map(run, mesh=mesh, in_specs=in_specs, out_specs=out_specs, check_vma=False)
```

```python
import functools

import jax
import jax.numpy as jnp
from jax import lax
from jax.experimental import pallas as pl
from jax.experimental.pallas import tpu as pltpu
from jax.sharding import PartitionSpec as P

MESH = pl.DeviceIdType.MESH
QUARTERS = 4
LANES = 256
FIELDS = (231, 186, 93)
DRAWS = (235, 85, 190)
MOTIONS = (231, 154, 125)


def each(start, stop, step):
    if stop - start <= 8:
        for i in range(start, stop):
            step(i)
    else:
        lax.fori_loop(start, stop, lambda i, carry: (step(i), carry)[1], 0)


def kernel(
    n_comp, n_site,
    factors, normals_h, loadings_h, mean_ln, sigma, got_m,
    weights, normals, loadings, drawn, mean_v, sigma_v, mix, sent_f, got_f, sent_m,
    w_sem, in_sem, d_send, d_pass, d_recv, f_send, f_recv, m_send, m_recv, keep_sem,
):
    me_c, me_s = lax.axis_index("comp"), lax.axis_index("site")
    ks, rows, rank = normals.shape
    periods, comps = loadings.shape
    s_dev = factors.shape[2]
    chunks = s_dev // LANES
    groups = n_site // 2 // n_comp
    chips = n_site // 2
    deep = rank // QUARTERS
    f32, bf16 = jnp.float32, jnp.bfloat16

    def load_w(t, k):
        lanes = pl.ds(t * LANES, LANES)
        return pltpu.make_async_copy(
            factors.at[k, :, lanes], weights.at[t, k], w_sem.at[t, k]
        )

    mean_copy = pltpu.make_async_copy(mean_ln, mean_v, in_sem.at[0])
    sigma_copy = pltpu.make_async_copy(sigma, sigma_v, in_sem.at[1])
    normals_copy = pltpu.make_async_copy(normals_h, normals, in_sem.at[2])
    loadings_copy = pltpu.make_async_copy(loadings_h, loadings, in_sem.at[3])
    normals_copy.start()

    barrier = pltpu.get_barrier_semaphore()

    def greet_s(d):
        pl.semaphore_signal(
            barrier, inc=1, device_id={"site": me_s ^ d}, device_id_type=MESH
        )

    def greet_c(d):
        pl.semaphore_signal(
            barrier, inc=1, device_id={"comp": me_c ^ d}, device_id_type=MESH
        )

    each(1, n_site, lambda d: greet_s(n_site - d))
    each(1, n_comp, lambda d: greet_c(n_comp - d))

    loadings_copy.start()
    for t in range(chunks):
        for k in range(ks):
            load_w(t, k).start()
    mean_copy.start()
    sigma_copy.start()
    normals_copy.wait()

    for k in range(ks):
        x = normals[k].astype(f32)
        x = jnp.concatenate([x[:, q * deep:(q + 1) * deep] for q in range(QUARTERS)], axis=0)
        drawn[me_s, 16 * k:16 * (k + 1), :] = x.astype(bf16)

    pl.semaphore_wait(barrier, n_site - 1 + n_comp - 1)

    pairs = ks // 2

    def draws(slot, send_sem, peer):
        return pltpu.make_async_remote_copy(
            src_ref=drawn.at[slot], dst_ref=drawn.at[slot],
            send_sem=send_sem, recv_sem=d_recv.at[slot],
            device_id={"site": peer}, device_id_type=MESH,
        )

    def across(d):
        return draws(me_s, d_send.at[d], me_s ^ (2 * d))

    def beside(d):
        return draws(me_s ^ (2 * d), d_pass.at[d], me_s ^ 1)

    def from_beside(d):
        return draws(me_s ^ (2 * d) ^ 1, d_pass.at[d], me_s ^ 1)

    def pick(table, at):
        return table // lax.shift_left(1, at * 2) % 4

    if chips == 4:
        first, second, last = (pick(table, me_s // 2) for table in DRAWS)
        across(first).start()
        across(second).start()
    else:
        each(1, chips, lambda d: across(chips - d).start())
    beside(0).start()

    spread = (
        lax.broadcasted_iota(jnp.int32, (comps, comps * 8), 1) >> 3
        == lax.broadcasted_iota(jnp.int32, (comps, comps * 8), 0)
    ).astype(f32).astype(bf16)
    turn = lax.broadcasted_iota(jnp.int32, (periods, comps * 8), 1) & 7
    loadings_copy.wait()
    rest = loadings[...]
    for i in range(3):
        term = rest.astype(bf16)
        rest = rest - term.astype(f32)
        wide = jnp.dot(term, spread, preferred_element_type=f32)
        full = jnp.concatenate([jnp.where(turn == r, wide, 0.0) for r in range(8)], axis=0)
        mix[i * periods * 8:(i + 1) * periods * 8, :] = full.astype(bf16)

    def pass_on(d):
        beside(d).wait_recv()
        beside(d).start()

    quarter = (lax.broadcasted_iota(jnp.int32, (n_site * 16, deep), 0) >> 2) & 3
    low = lax.broadcasted_iota(jnp.int32, (chips, 8, LANES), 1) < 4

    def product(t, k):
        x = drawn[:, 16 * k:16 * (k + 1), :].reshape(n_site * 16, deep).astype(f32)
        lhs = jnp.concatenate(
            [jnp.where(quarter == q, x, 0.0).astype(bf16) for q in range(QUARTERS)], axis=1
        )
        y = jnp.dot(lhs, weights[t, k], preferred_element_type=f32)
        y = y.reshape(n_site, 2, 8, LANES)
        y = y[:, 0] + y[:, 1]
        y = y + pltpu.roll(y, 4, 1)
        y = y.reshape(chips, 2, 8, LANES)
        return jnp.where(low, y[:, 0], y[:, 1])

    def f_copy(t, d):
        peer = me_c ^ d
        at = pl.ds(pl.multiple_of(me_c * ks * 8, 16), ks * 8)
        return pltpu.make_async_remote_copy(
            src_ref=sent_f.at[t, peer], dst_ref=got_f.at[t, :, at, :],
            send_sem=f_send.at[t, d], recv_sem=f_recv.at[t, d],
            device_id={"comp": peer}, device_id_type=MESH,
        )

    def fields(j, t):
        both = jnp.concatenate([product(t, 2 * j), product(t, 2 * j + 1)], axis=1).astype(bf16)
        sent_f[t, :, :, 16 * j:16 * (j + 1), :] = both.reshape(n_comp, groups, 16, LANES)

    def send_fields(t):
        for table in FIELDS:
            f_copy(t, pick(table, me_c)).start()
        at = pl.ds(pl.multiple_of(me_c * ks * 8, 16), ks * 8)
        got_f[t, :, at, :] = sent_f[t, me_c]

    def m_copy(t, d):
        peer = me_s ^ d
        return pltpu.make_async_remote_copy(
            src_ref=sent_m.at[t, peer], dst_ref=got_m.at[t, me_s],
            send_sem=m_send.at[t, d], recv_sem=m_recv.at[t, d],
            device_id={"site": peer}, device_id_type=MESH,
        )

    def push(t, tables):
        for table in tables:
            d = pick(table, me_s // 2) * 2
            m_copy(t, d + 1).start()
            m_copy(t, d).start()

    def push_rest(t):
        if chips == 4:
            push(t, MOTIONS[2:])
            m_copy(t, 1).start()

    def motions(t):
        for d in range(1, n_comp):
            f_copy(t, d).wait_recv()
        mean = mean_v[:, t * LANES:(t + 1) * LANES]
        dev = sigma_v[:, t * LANES:(t + 1) * LANES]
        n = periods * 8

        def one(g):
            e = jnp.dot(mix[...], got_f[t, g], preferred_element_type=f32)
            e = (e[2 * n:] + e[n:2 * n]) + e[:n]
            m = mean[None] + dev[None] * e.reshape(8, periods, LANES)
            m = jnp.concatenate([m[:, :, :LANES // 2], m[:, :, LANES // 2:]], axis=1)
            sent_m[t, pl.ds(8 * g, 8)] = m.astype(bf16)

        each(0, groups, one)
        if chips == 4:
            push(t, MOTIONS[:2])
        else:
            each(1, n_site, lambda d: m_copy(t, n_site - d).start())
        m_keep(t).start()

    def m_keep(t):
        return pltpu.make_async_copy(sent_m.at[t, me_s], got_m.at[t, me_s], keep_sem.at[t])

    if chips == 4:
        across(first).wait_send()
        across(last).start()
    for t in range(chunks):
        for k in range(ks):
            load_w(t, k).wait()
    each(1, chips, pass_on)
    each(0, chips, lambda d: from_beside(d).wait_recv())
    for t in range(chunks):
        for j in range(pairs):
            fields(j, t)
        send_fields(t)
    mean_copy.wait()
    sigma_copy.wait()
    for t in range(chunks):
        motions(t)
    for t in range(chunks):
        push_rest(t)

    if chips == 4:
        across(second).wait_send()
        across(last).wait_send()
    else:
        each(1, chips, lambda d: across(d).wait_send())
    each(0, chips, lambda d: beside(d).wait_send())
    for t in range(chunks):
        for d in range(1, n_comp):
            f_copy(t, d).wait_send()
    for t in range(chunks):
        m_keep(t).wait()
        each(1, n_site, lambda d: m_copy(t, d).wait_send())
    for t in range(chunks):
        each(1, n_site, lambda d: m_copy(t, d).wait_recv())


def arrange(blocks, out):
    chunks, slabs, rows, half = blocks.shape
    periods = rows // 2

    def one(s):
        for t in range(chunks):
            x = blocks[t, s].astype(jnp.float32)
            for h in range(2):
                at = pl.multiple_of((s * chunks + t) * 2 * half + h * half, half)
                out[0, :, pl.ds(at, half)] = x[h * periods:(h + 1) * periods].astype(out.dtype)

    each(0, slabs, one)


def body(n_comp, n_site, factors, normals, loadings, mean_ln, sigma):
    ks, rank, s_dev = factors.shape
    rows = normals.shape[1]
    periods, comps = loadings.shape
    groups = n_site // 2 // n_comp
    chunks = s_dev // LANES
    assert rows == 4 and n_comp == rows and n_site % (2 * n_comp) == 0
    assert n_site & (n_site - 1) == 0
    assert ks % 2 == 0 and periods % 8 == 0 and s_dev % LANES == 0
    bf16 = jnp.bfloat16
    dma = pltpu.SemaphoreType.DMA
    any_ = pl.BlockSpec(memory_space=pl.ANY)
    blocks = pl.pallas_call(
        functools.partial(kernel, n_comp, n_site),
        out_shape=pltpu.VMEM((chunks, n_site, 2 * periods, LANES // 2), bf16),
        in_specs=[any_] * 5,
        out_specs=any_,
        scratch_shapes=[
            pltpu.VMEM((chunks, ks, rank, LANES), bf16),
            pltpu.VMEM(normals.shape, bf16),
            pltpu.VMEM(loadings.shape, jnp.float32),
            pltpu.VMEM((n_site, ks * 16, rank // QUARTERS), bf16),
            pltpu.VMEM((periods, s_dev), jnp.float32),
            pltpu.VMEM((periods, s_dev), jnp.float32),
            pltpu.VMEM((3 * periods * 8, comps * 8), bf16),
            pltpu.VMEM((chunks, n_comp, groups, ks * 8, LANES), bf16),
            pltpu.VMEM((chunks, groups, comps * 8, LANES), bf16),
            pltpu.VMEM((chunks, n_site, 2 * periods, LANES // 2), bf16),
            dma((chunks, ks)), dma((4,)),
            dma((n_site // 2,)), dma((n_site // 2,)), dma((n_site,)),
            dma((chunks, n_comp)), dma((chunks, n_comp)),
            dma((chunks, n_site)), dma((chunks, n_site)), dma((chunks,)),
        ],
        compiler_params=pltpu.CompilerParams(
            collective_id=0, has_side_effects=True, vmem_limit_bytes=40 * 1024 * 1024
        ),
        cost_estimate=pl.CostEstimate(
            flops=2 * ks * rows * n_site * rank * s_dev,
            bytes_accessed=2 * ks * rank * s_dev, transcendentals=0,
        ),
    )(*(pltpu.with_memory_space_constraint(x, pltpu.HBM) for x in (factors, normals, loadings, mean_ln, sigma)))
    return pl.pallas_call(
        arrange,
        out_shape=jax.ShapeDtypeStruct((1, periods, n_site * s_dev), bf16),
        in_specs=[pl.BlockSpec(memory_space=pltpu.VMEM)],
        out_specs=pl.BlockSpec(memory_space=pltpu.VMEM),
        compiler_params=pltpu.CompilerParams(vmem_limit_bytes=40 * 1024 * 1024),
    )(pltpu.with_memory_space_constraint(blocks, pltpu.VMEM))


def solution(mesh):
    in_specs = (
        P("comp", None, "site"),
        P("comp", "site", None),
        P(),
        P(None, "site"),
        P(None, "site"),
    )
    out_specs = P(("comp", "site"), None, None)
    run = functools.partial(body, mesh.shape["comp"], mesh.shape["site"])
    return jax.shard_map(run, mesh=mesh, in_specs=in_specs, out_specs=out_specs, check_vma=False)
```

```python
import functools

import jax
import jax.numpy as jnp
from jax import lax
from jax.experimental import pallas as pl
from jax.experimental.pallas import tpu as pltpu
from jax.sharding import PartitionSpec as P

MESH = pl.DeviceIdType.MESH
QUARTERS = 4
LANES = 256
FIELDS = (231, 186, 93)
DRAWS = (235, 85, 190)
MOTIONS = (231, 154, 125)


def each(start, stop, step):
    if stop - start <= 8:
        for i in range(start, stop):
            step(i)
    else:
        lax.fori_loop(start, stop, lambda i, carry: (step(i), carry)[1], 0)


def kernel(
    n_comp, n_site,
    factors, normals_h, loadings_h, mean_ln, sigma, got_m,
    weights, normals, loadings, drawn, mean_v, sigma_v, mix, sent_f, got_f, sent_m,
    w_sem, in_sem, d_send, d_pass, d_recv, f_send, f_recv, m_send, m_recv, keep_sem,
):
    me_c, me_s = lax.axis_index("comp"), lax.axis_index("site")
    ks, rows, rank = normals.shape
    periods, comps = loadings.shape
    s_dev = factors.shape[2]
    chunks = s_dev // LANES
    groups = n_site // 2 // n_comp
    chips = n_site // 2
    deep = rank // QUARTERS
    f32, bf16 = jnp.float32, jnp.bfloat16

    def load_w(t, k):
        lanes = pl.ds(t * LANES, LANES)
        return pltpu.make_async_copy(
            factors.at[k, :, lanes], weights.at[t, k], w_sem.at[t, k]
        )

    mean_copy = pltpu.make_async_copy(mean_ln, mean_v, in_sem.at[0])
    sigma_copy = pltpu.make_async_copy(sigma, sigma_v, in_sem.at[1])
    normals_copy = pltpu.make_async_copy(normals_h, normals, in_sem.at[2])
    loadings_copy = pltpu.make_async_copy(loadings_h, loadings, in_sem.at[3])
    normals_copy.start()

    barrier = pltpu.get_barrier_semaphore()

    def greet_s(d):
        pl.semaphore_signal(
            barrier, inc=1, device_id={"site": me_s ^ d}, device_id_type=MESH
        )

    def greet_c(d):
        pl.semaphore_signal(
            barrier, inc=1, device_id={"comp": me_c ^ d}, device_id_type=MESH
        )

    each(1, n_site, lambda d: greet_s(n_site - d))
    each(1, n_comp, lambda d: greet_c(n_comp - d))

    loadings_copy.start()
    for t in range(chunks):
        for k in range(ks):
            load_w(t, k).start()
    mean_copy.start()
    sigma_copy.start()
    normals_copy.wait()

    for k in range(ks):
        x = normals[k].astype(f32)
        x = jnp.concatenate([x[:, q * deep:(q + 1) * deep] for q in range(QUARTERS)], axis=0)
        drawn[me_s, 16 * k:16 * (k + 1), :] = x.astype(bf16)

    pl.semaphore_wait(barrier, n_site - 1 + n_comp - 1)

    pairs = ks // 2

    def draws(slot, send_sem, peer):
        return pltpu.make_async_remote_copy(
            src_ref=drawn.at[slot], dst_ref=drawn.at[slot],
            send_sem=send_sem, recv_sem=d_recv.at[slot],
            device_id={"site": peer}, device_id_type=MESH,
        )

    def across(d):
        return draws(me_s, d_send.at[d], me_s ^ (2 * d))

    def beside(d):
        return draws(me_s ^ (2 * d), d_pass.at[d], me_s ^ 1)

    def from_beside(d):
        return draws(me_s ^ (2 * d) ^ 1, d_pass.at[d], me_s ^ 1)

    def pick(table, at):
        return table // lax.shift_left(1, at * 2) % 4

    if chips == 4:
        first, second, last = (pick(table, me_s // 2) for table in DRAWS)
        across(first).start()
        across(second).start()
    else:
        each(1, chips, lambda d: across(chips - d).start())
    beside(0).start()

    spread = (
        lax.broadcasted_iota(jnp.int32, (comps, comps * 8), 1) >> 3
        == lax.broadcasted_iota(jnp.int32, (comps, comps * 8), 0)
    ).astype(f32).astype(bf16)
    turn = lax.broadcasted_iota(jnp.int32, (periods, comps * 8), 1) & 7
    loadings_copy.wait()
    rest = loadings[...]
    for i in range(3):
        term = rest.astype(bf16)
        rest = rest - term.astype(f32)
        wide = jnp.dot(term, spread, preferred_element_type=f32)
        full = jnp.concatenate([jnp.where(turn == r, wide, 0.0) for r in range(8)], axis=0)
        mix[i * periods * 8:(i + 1) * periods * 8, :] = full.astype(bf16)

    def pass_on(d):
        beside(d).wait_recv()
        beside(d).start()

    quarter = (lax.broadcasted_iota(jnp.int32, (n_site * 16, deep), 0) >> 2) & 3
    low = lax.broadcasted_iota(jnp.int32, (chips, 8, LANES), 1) < 4

    def product(t, k):
        x = drawn[:, 16 * k:16 * (k + 1), :].reshape(n_site * 16, deep).astype(f32)
        lhs = jnp.concatenate(
            [jnp.where(quarter == q, x, 0.0).astype(bf16) for q in range(QUARTERS)], axis=1
        )
        y = jnp.dot(lhs, weights[t, k], preferred_element_type=f32)
        y = y.reshape(n_site, 2, 8, LANES)
        y = y[:, 0] + y[:, 1]
        y = y + pltpu.roll(y, 4, 1)
        y = y.reshape(chips, 2, 8, LANES)
        return jnp.where(low, y[:, 0], y[:, 1])

    def f_copy(t, d):
        peer = me_c ^ d
        at = pl.ds(pl.multiple_of(me_c * ks * 8, 16), ks * 8)
        return pltpu.make_async_remote_copy(
            src_ref=sent_f.at[t, peer], dst_ref=got_f.at[t, :, at, :],
            send_sem=f_send.at[t, d], recv_sem=f_recv.at[t, d],
            device_id={"comp": peer}, device_id_type=MESH,
        )

    def fields(j, t):
        both = jnp.concatenate([product(t, 2 * j), product(t, 2 * j + 1)], axis=1).astype(bf16)
        sent_f[t, :, :, 16 * j:16 * (j + 1), :] = both.reshape(n_comp, groups, 16, LANES)

    def push_fields(t, tables):
        for table in tables:
            f_copy(t, pick(table, me_c)).start()

    def send_fields(t):
        push_fields(t, FIELDS[:1])
        at = pl.ds(pl.multiple_of(me_c * ks * 8, 16), ks * 8)
        got_f[t, :, at, :] = sent_f[t, me_c]

    def m_copy(t, d):
        peer = me_s ^ d
        return pltpu.make_async_remote_copy(
            src_ref=sent_m.at[t, peer], dst_ref=got_m.at[t, me_s],
            send_sem=m_send.at[t, d], recv_sem=m_recv.at[t, d],
            device_id={"site": peer}, device_id_type=MESH,
        )

    def push(t, tables):
        for table in tables:
            d = pick(table, me_s // 2) * 2
            m_copy(t, d + me_s % 2).start()
            m_copy(t, d + 1 - me_s % 2).start()

    def push_rest(t):
        if chips == 4:
            push(t, MOTIONS[2:])
            m_copy(t, 1).start()

    def motions(t):
        for d in range(1, n_comp):
            f_copy(t, d).wait_recv()
        mean = mean_v[:, t * LANES:(t + 1) * LANES]
        dev = sigma_v[:, t * LANES:(t + 1) * LANES]
        n = periods * 8

        def one(g):
            e = jnp.dot(mix[...], got_f[t, g], preferred_element_type=f32)
            e = (e[2 * n:] + e[n:2 * n]) + e[:n]
            m = mean[None] + dev[None] * e.reshape(8, periods, LANES)
            m = jnp.concatenate([m[:, :, :LANES // 2], m[:, :, LANES // 2:]], axis=1)
            sent_m[t, pl.ds(8 * g, 8)] = m.astype(bf16)

        each(0, groups, one)
        if chips == 4:
            push(t, MOTIONS[:2])
        else:
            each(1, n_site, lambda d: m_copy(t, n_site - d).start())
        m_keep(t).start()

    def m_keep(t):
        return pltpu.make_async_copy(sent_m.at[t, me_s], got_m.at[t, me_s], keep_sem.at[t])

    if chips == 4:
        across(first).wait_send()
        across(last).start()
    for t in range(chunks):
        for k in range(ks):
            load_w(t, k).wait()
    each(1, chips, pass_on)
    each(0, chips, lambda d: from_beside(d).wait_recv())
    for t in range(chunks):
        for j in range(pairs):
            fields(j, t)
        send_fields(t)
        if t > 0:
            push_fields(t - 1, FIELDS[1:])
    push_fields(chunks - 1, FIELDS[1:])
    mean_copy.wait()
    sigma_copy.wait()
    for t in range(chunks):
        motions(t)
    for t in range(chunks):
        push_rest(t)

    if chips == 4:
        across(second).wait_send()
        across(last).wait_send()
    else:
        each(1, chips, lambda d: across(d).wait_send())
    each(0, chips, lambda d: beside(d).wait_send())
    for t in range(chunks):
        for d in range(1, n_comp):
            f_copy(t, d).wait_send()
    for t in range(chunks):
        m_keep(t).wait()
        each(1, n_site, lambda d: m_copy(t, d).wait_send())
    for t in range(chunks):
        each(1, n_site, lambda d: m_copy(t, d).wait_recv())


def arrange(blocks, out):
    chunks, slabs, rows, half = blocks.shape
    periods = rows // 2

    def one(s):
        for t in range(chunks):
            x = blocks[t, s].astype(jnp.float32)
            for h in range(2):
                at = pl.multiple_of((s * chunks + t) * 2 * half + h * half, half)
                out[0, :, pl.ds(at, half)] = x[h * periods:(h + 1) * periods].astype(out.dtype)

    each(0, slabs, one)


def body(n_comp, n_site, factors, normals, loadings, mean_ln, sigma):
    ks, rank, s_dev = factors.shape
    rows = normals.shape[1]
    periods, comps = loadings.shape
    groups = n_site // 2 // n_comp
    chunks = s_dev // LANES
    assert rows == 4 and n_comp == rows and n_site % (2 * n_comp) == 0
    assert n_site & (n_site - 1) == 0
    assert ks % 2 == 0 and periods % 8 == 0 and s_dev % LANES == 0
    bf16 = jnp.bfloat16
    dma = pltpu.SemaphoreType.DMA
    any_ = pl.BlockSpec(memory_space=pl.ANY)
    blocks = pl.pallas_call(
        functools.partial(kernel, n_comp, n_site),
        out_shape=pltpu.VMEM((chunks, n_site, 2 * periods, LANES // 2), bf16),
        in_specs=[any_] * 5,
        out_specs=any_,
        scratch_shapes=[
            pltpu.VMEM((chunks, ks, rank, LANES), bf16),
            pltpu.VMEM(normals.shape, bf16),
            pltpu.VMEM(loadings.shape, jnp.float32),
            pltpu.VMEM((n_site, ks * 16, rank // QUARTERS), bf16),
            pltpu.VMEM((periods, s_dev), jnp.float32),
            pltpu.VMEM((periods, s_dev), jnp.float32),
            pltpu.VMEM((3 * periods * 8, comps * 8), bf16),
            pltpu.VMEM((chunks, n_comp, groups, ks * 8, LANES), bf16),
            pltpu.VMEM((chunks, groups, comps * 8, LANES), bf16),
            pltpu.VMEM((chunks, n_site, 2 * periods, LANES // 2), bf16),
            dma((chunks, ks)), dma((4,)),
            dma((n_site // 2,)), dma((n_site // 2,)), dma((n_site,)),
            dma((chunks, n_comp)), dma((chunks, n_comp)),
            dma((chunks, n_site)), dma((chunks, n_site)), dma((chunks,)),
        ],
        compiler_params=pltpu.CompilerParams(
            collective_id=0, has_side_effects=True, vmem_limit_bytes=40 * 1024 * 1024
        ),
        cost_estimate=pl.CostEstimate(
            flops=2 * ks * rows * n_site * rank * s_dev,
            bytes_accessed=2 * ks * rank * s_dev, transcendentals=0,
        ),
    )(*(pltpu.with_memory_space_constraint(x, pltpu.HBM) for x in (factors, normals, loadings, mean_ln, sigma)))
    return pl.pallas_call(
        arrange,
        out_shape=jax.ShapeDtypeStruct((1, periods, n_site * s_dev), bf16),
        in_specs=[pl.BlockSpec(memory_space=pltpu.VMEM)],
        out_specs=pl.BlockSpec(memory_space=pltpu.VMEM),
        compiler_params=pltpu.CompilerParams(vmem_limit_bytes=40 * 1024 * 1024),
    )(pltpu.with_memory_space_constraint(blocks, pltpu.VMEM))


def solution(mesh):
    in_specs = (
        P("comp", None, "site"),
        P("comp", "site", None),
        P(),
        P(None, "site"),
        P(None, "site"),
    )
    out_specs = P(("comp", "site"), None, None)
    run = functools.partial(body, mesh.shape["comp"], mesh.shape["site"])
    return jax.shard_map(run, mesh=mesh, in_specs=in_specs, out_specs=out_specs, check_vma=False)
```

```python
import functools

import jax
import jax.numpy as jnp
from jax import lax
from jax.experimental import pallas as pl
from jax.experimental.pallas import tpu as pltpu
from jax.sharding import PartitionSpec as P

MESH = pl.DeviceIdType.MESH
QUARTERS = 4
LANES = 256
FIELDS = (231, 186, 93)
DRAWS = (155, 117, 238)
MOTIONS = (231, 154, 125)


def each(start, stop, step):
    if stop - start <= 8:
        for i in range(start, stop):
            step(i)
    else:
        lax.fori_loop(start, stop, lambda i, carry: (step(i), carry)[1], 0)


def kernel(
    n_comp, n_site,
    factors, normals_h, loadings_h, mean_ln, sigma, got_m,
    weights, normals, loadings, drawn, mean_v, sigma_v, mix, sent_f, got_f, sent_m,
    w_sem, in_sem, d_send, d_pass, d_recv, f_send, f_recv, m_send, m_recv, keep_sem,
):
    me_c, me_s = lax.axis_index("comp"), lax.axis_index("site")
    ks, rows, rank = normals.shape
    periods, comps = loadings.shape
    s_dev = factors.shape[2]
    chunks = s_dev // LANES
    groups = n_site // 2 // n_comp
    chips = n_site // 2
    deep = rank // QUARTERS
    f32, bf16 = jnp.float32, jnp.bfloat16

    def load_w(t, k):
        lanes = pl.ds(t * LANES, LANES)
        return pltpu.make_async_copy(
            factors.at[k, :, lanes], weights.at[t, k], w_sem.at[t, k]
        )

    mean_copy = pltpu.make_async_copy(mean_ln, mean_v, in_sem.at[0])
    sigma_copy = pltpu.make_async_copy(sigma, sigma_v, in_sem.at[1])
    normals_copy = pltpu.make_async_copy(normals_h, normals, in_sem.at[2])
    loadings_copy = pltpu.make_async_copy(loadings_h, loadings, in_sem.at[3])
    normals_copy.start()

    barrier = pltpu.get_barrier_semaphore()

    def greet_s(d):
        pl.semaphore_signal(
            barrier, inc=1, device_id={"site": me_s ^ d}, device_id_type=MESH
        )

    def greet_c(d):
        pl.semaphore_signal(
            barrier, inc=1, device_id={"comp": me_c ^ d}, device_id_type=MESH
        )

    each(1, n_site, lambda d: greet_s(n_site - d))
    each(1, n_comp, lambda d: greet_c(n_comp - d))

    loadings_copy.start()
    for t in range(chunks):
        for k in range(ks):
            load_w(t, k).start()
    mean_copy.start()
    sigma_copy.start()
    normals_copy.wait()

    for k in range(ks):
        x = normals[k].astype(f32)
        x = jnp.concatenate([x[:, q * deep:(q + 1) * deep] for q in range(QUARTERS)], axis=0)
        drawn[me_s, 16 * k:16 * (k + 1), :] = x.astype(bf16)

    pl.semaphore_wait(barrier, n_site - 1 + n_comp - 1)

    pairs = ks // 2

    def draws(slot, send_sem, peer):
        return pltpu.make_async_remote_copy(
            src_ref=drawn.at[slot], dst_ref=drawn.at[slot],
            send_sem=send_sem, recv_sem=d_recv.at[slot],
            device_id={"site": peer}, device_id_type=MESH,
        )

    def across(d):
        return draws(me_s, d_send.at[d], me_s ^ (2 * d))

    def beside(d):
        return draws(me_s ^ (2 * d), d_pass.at[d], me_s ^ 1)

    def from_beside(d):
        return draws(me_s ^ (2 * d) ^ 1, d_pass.at[d], me_s ^ 1)

    def pick(table, at):
        return table // lax.shift_left(1, at * 2) % 4

    if chips == 4:
        first, second, last = (pick(table, me_s // 2) for table in DRAWS)
        across(first).start()
        across(second).start()
    else:
        each(1, chips, lambda d: across(chips - d).start())
    beside(0).start()

    spread = (
        lax.broadcasted_iota(jnp.int32, (comps, comps * 8), 1) >> 3
        == lax.broadcasted_iota(jnp.int32, (comps, comps * 8), 0)
    ).astype(f32).astype(bf16)
    turn = lax.broadcasted_iota(jnp.int32, (periods, comps * 8), 1) & 7
    loadings_copy.wait()
    rest = loadings[...]
    for i in range(3):
        term = rest.astype(bf16)
        rest = rest - term.astype(f32)
        wide = jnp.dot(term, spread, preferred_element_type=f32)
        full = jnp.concatenate([jnp.where(turn == r, wide, 0.0) for r in range(8)], axis=0)
        mix[i * periods * 8:(i + 1) * periods * 8, :] = full.astype(bf16)

    def pass_on(d):
        beside(d).wait_recv()
        beside(d).start()

    quarter = (lax.broadcasted_iota(jnp.int32, (n_site * 16, deep), 0) >> 2) & 3
    low = lax.broadcasted_iota(jnp.int32, (chips, 8, LANES), 1) < 4

    def product(t, k):
        x = drawn[:, 16 * k:16 * (k + 1), :].reshape(n_site * 16, deep).astype(f32)
        lhs = jnp.concatenate(
            [jnp.where(quarter == q, x, 0.0).astype(bf16) for q in range(QUARTERS)], axis=1
        )
        y = jnp.dot(lhs, weights[t, k], preferred_element_type=f32)
        y = y.reshape(n_site, 2, 8, LANES)
        y = y[:, 0] + y[:, 1]
        y = y + pltpu.roll(y, 4, 1)
        y = y.reshape(chips, 2, 8, LANES)
        return jnp.where(low, y[:, 0], y[:, 1])

    def f_copy(t, d):
        peer = me_c ^ d
        at = pl.ds(pl.multiple_of(me_c * ks * 8, 16), ks * 8)
        return pltpu.make_async_remote_copy(
            src_ref=sent_f.at[t, peer], dst_ref=got_f.at[t, :, at, :],
            send_sem=f_send.at[t, d], recv_sem=f_recv.at[t, d],
            device_id={"comp": peer}, device_id_type=MESH,
        )

    def fields(j, t):
        both = jnp.concatenate([product(t, 2 * j), product(t, 2 * j + 1)], axis=1).astype(bf16)
        sent_f[t, :, :, 16 * j:16 * (j + 1), :] = both.reshape(n_comp, groups, 16, LANES)

    def push_fields(t, tables):
        for table in tables:
            f_copy(t, pick(table, me_c)).start()

    def send_fields(t):
        push_fields(t, FIELDS[:1])
        at = pl.ds(pl.multiple_of(me_c * ks * 8, 16), ks * 8)
        got_f[t, :, at, :] = sent_f[t, me_c]

    def m_copy(t, d):
        peer = me_s ^ d
        return pltpu.make_async_remote_copy(
            src_ref=sent_m.at[t, peer], dst_ref=got_m.at[t, me_s],
            send_sem=m_send.at[t, d], recv_sem=m_recv.at[t, d],
            device_id={"site": peer}, device_id_type=MESH,
        )

    def push(t, tables):
        for table in tables:
            d = pick(table, me_s // 2) * 2
            m_copy(t, d + me_s % 2).start()
            m_copy(t, d + 1 - me_s % 2).start()

    def push_rest(t):
        if chips == 4:
            push(t, MOTIONS[2:])
            m_copy(t, 1).start()

    def motions(t):
        for d in range(1, n_comp):
            f_copy(t, d).wait_recv()
        mean = mean_v[:, t * LANES:(t + 1) * LANES]
        dev = sigma_v[:, t * LANES:(t + 1) * LANES]
        n = periods * 8

        def one(g):
            e = jnp.dot(mix[...], got_f[t, g], preferred_element_type=f32)
            e = (e[2 * n:] + e[n:2 * n]) + e[:n]
            m = mean[None] + dev[None] * e.reshape(8, periods, LANES)
            m = jnp.concatenate([m[:, :, :LANES // 2], m[:, :, LANES // 2:]], axis=1)
            sent_m[t, pl.ds(8 * g, 8)] = m.astype(bf16)

        each(0, groups, one)
        if chips == 4:
            push(t, MOTIONS[:2])
        else:
            each(1, n_site, lambda d: m_copy(t, n_site - d).start())
        m_keep(t).start()

    def m_keep(t):
        return pltpu.make_async_copy(sent_m.at[t, me_s], got_m.at[t, me_s], keep_sem.at[t])

    if chips == 4:
        across(second).wait_send()
        across(last).start()
    for t in range(chunks):
        for k in range(ks):
            load_w(t, k).wait()
    each(1, chips, pass_on)
    each(0, chips, lambda d: from_beside(d).wait_recv())
    for t in range(chunks):
        for j in range(pairs):
            fields(j, t)
        send_fields(t)
        if t > 0:
            push_fields(t - 1, FIELDS[1:])
    push_fields(chunks - 1, FIELDS[1:])
    mean_copy.wait()
    sigma_copy.wait()
    for t in range(chunks):
        motions(t)
    for t in range(chunks):
        push_rest(t)

    if chips == 4:
        across(first).wait_send()
        across(last).wait_send()
    else:
        each(1, chips, lambda d: across(d).wait_send())
    each(0, chips, lambda d: beside(d).wait_send())
    for t in range(chunks):
        for d in range(1, n_comp):
            f_copy(t, d).wait_send()
    for t in range(chunks):
        m_keep(t).wait()
        each(1, n_site, lambda d: m_copy(t, d).wait_send())
    for t in range(chunks):
        each(1, n_site, lambda d: m_copy(t, d).wait_recv())


def arrange(blocks, out):
    chunks, slabs, rows, half = blocks.shape
    periods = rows // 2

    def one(s):
        for t in range(chunks):
            x = blocks[t, s].astype(jnp.float32)
            for h in range(2):
                at = pl.multiple_of((s * chunks + t) * 2 * half + h * half, half)
                out[0, :, pl.ds(at, half)] = x[h * periods:(h + 1) * periods].astype(out.dtype)

    each(0, slabs, one)


def body(n_comp, n_site, factors, normals, loadings, mean_ln, sigma):
    ks, rank, s_dev = factors.shape
    rows = normals.shape[1]
    periods, comps = loadings.shape
    groups = n_site // 2 // n_comp
    chunks = s_dev // LANES
    assert rows == 4 and n_comp == rows and n_site % (2 * n_comp) == 0
    assert n_site & (n_site - 1) == 0
    assert ks % 2 == 0 and periods % 8 == 0 and s_dev % LANES == 0
    bf16 = jnp.bfloat16
    dma = pltpu.SemaphoreType.DMA
    any_ = pl.BlockSpec(memory_space=pl.ANY)
    blocks = pl.pallas_call(
        functools.partial(kernel, n_comp, n_site),
        out_shape=pltpu.VMEM((chunks, n_site, 2 * periods, LANES // 2), bf16),
        in_specs=[any_] * 5,
        out_specs=any_,
        scratch_shapes=[
            pltpu.VMEM((chunks, ks, rank, LANES), bf16),
            pltpu.VMEM(normals.shape, bf16),
            pltpu.VMEM(loadings.shape, jnp.float32),
            pltpu.VMEM((n_site, ks * 16, rank // QUARTERS), bf16),
            pltpu.VMEM((periods, s_dev), jnp.float32),
            pltpu.VMEM((periods, s_dev), jnp.float32),
            pltpu.VMEM((3 * periods * 8, comps * 8), bf16),
            pltpu.VMEM((chunks, n_comp, groups, ks * 8, LANES), bf16),
            pltpu.VMEM((chunks, groups, comps * 8, LANES), bf16),
            pltpu.VMEM((chunks, n_site, 2 * periods, LANES // 2), bf16),
            dma((chunks, ks)), dma((4,)),
            dma((n_site // 2,)), dma((n_site // 2,)), dma((n_site,)),
            dma((chunks, n_comp)), dma((chunks, n_comp)),
            dma((chunks, n_site)), dma((chunks, n_site)), dma((chunks,)),
        ],
        compiler_params=pltpu.CompilerParams(
            collective_id=0, has_side_effects=True, vmem_limit_bytes=40 * 1024 * 1024
        ),
        cost_estimate=pl.CostEstimate(
            flops=2 * ks * rows * n_site * rank * s_dev,
            bytes_accessed=2 * ks * rank * s_dev, transcendentals=0,
        ),
    )(*(pltpu.with_memory_space_constraint(x, pltpu.HBM) for x in (factors, normals, loadings, mean_ln, sigma)))
    return pl.pallas_call(
        arrange,
        out_shape=jax.ShapeDtypeStruct((1, periods, n_site * s_dev), bf16),
        in_specs=[pl.BlockSpec(memory_space=pltpu.VMEM)],
        out_specs=pl.BlockSpec(memory_space=pltpu.VMEM),
        compiler_params=pltpu.CompilerParams(vmem_limit_bytes=40 * 1024 * 1024),
    )(pltpu.with_memory_space_constraint(blocks, pltpu.VMEM))


def solution(mesh):
    in_specs = (
        P("comp", None, "site"),
        P("comp", "site", None),
        P(),
        P(None, "site"),
        P(None, "site"),
    )
    out_specs = P(("comp", "site"), None, None)
    run = functools.partial(body, mesh.shape["comp"], mesh.shape["site"])
    return jax.shard_map(run, mesh=mesh, in_specs=in_specs, out_specs=out_specs, check_vma=False)
```

```python
import functools

import jax
import jax.numpy as jnp
from jax import lax
from jax.experimental import pallas as pl
from jax.experimental.pallas import tpu as pltpu
from jax.sharding import PartitionSpec as P

MESH = pl.DeviceIdType.MESH
QUARTERS = 4
LANES = 256
FIELDS = (231, 186, 93)
DRAWS = (155, 117, 238)
MOTIONS = (231, 154, 125)


def each(start, stop, step):
    if stop - start <= 8:
        for i in range(start, stop):
            step(i)
    else:
        lax.fori_loop(start, stop, lambda i, carry: (step(i), carry)[1], 0)


def kernel(
    n_comp, n_site,
    factors, normals_h, loadings_h, mean_ln, sigma, got_m,
    weights, normals, loadings, drawn, mean_v, sigma_v, mix, sent_f, got_f, sent_m,
    w_sem, in_sem, d_send, d_pass, d_recv, f_send, f_recv, m_send, m_recv, keep_sem,
):
    me_c, me_s = lax.axis_index("comp"), lax.axis_index("site")
    ks, rows, rank = normals.shape
    periods, comps = loadings.shape
    s_dev = factors.shape[2]
    chunks = s_dev // LANES
    groups = n_site // 2 // n_comp
    chips = n_site // 2
    deep = rank // QUARTERS
    f32, bf16 = jnp.float32, jnp.bfloat16

    def load_w(t, k):
        lanes = pl.ds(t * LANES, LANES)
        return pltpu.make_async_copy(
            factors.at[k, :, lanes], weights.at[t, k], w_sem.at[t, k]
        )

    mean_copy = pltpu.make_async_copy(mean_ln, mean_v, in_sem.at[0])
    sigma_copy = pltpu.make_async_copy(sigma, sigma_v, in_sem.at[1])
    normals_copy = pltpu.make_async_copy(normals_h, normals, in_sem.at[2])
    loadings_copy = pltpu.make_async_copy(loadings_h, loadings, in_sem.at[3])
    normals_copy.start()

    barrier = pltpu.get_barrier_semaphore()

    def greet_s(d):
        pl.semaphore_signal(
            barrier, inc=1, device_id={"site": me_s ^ d}, device_id_type=MESH
        )

    def greet_c(d):
        pl.semaphore_signal(
            barrier, inc=1, device_id={"comp": me_c ^ d}, device_id_type=MESH
        )

    each(1, n_site, lambda d: greet_s(n_site - d))
    each(1, n_comp, lambda d: greet_c(n_comp - d))

    normals_copy.wait()
    loadings_copy.start()
    for t in range(chunks):
        for k in range(ks):
            load_w(t, k).start()
    mean_copy.start()
    sigma_copy.start()

    for k in range(ks):
        x = normals[k].astype(f32)
        x = jnp.concatenate([x[:, q * deep:(q + 1) * deep] for q in range(QUARTERS)], axis=0)
        drawn[me_s, 16 * k:16 * (k + 1), :] = x.astype(bf16)

    pl.semaphore_wait(barrier, n_site - 1 + n_comp - 1)

    pairs = ks // 2

    def draws(slot, send_sem, peer):
        return pltpu.make_async_remote_copy(
            src_ref=drawn.at[slot], dst_ref=drawn.at[slot],
            send_sem=send_sem, recv_sem=d_recv.at[slot],
            device_id={"site": peer}, device_id_type=MESH,
        )

    def across(d):
        return draws(me_s, d_send.at[d], me_s ^ (2 * d))

    def beside(d):
        return draws(me_s ^ (2 * d), d_pass.at[d], me_s ^ 1)

    def from_beside(d):
        return draws(me_s ^ (2 * d) ^ 1, d_pass.at[d], me_s ^ 1)

    def pick(table, at):
        return table // lax.shift_left(1, at * 2) % 4

    if chips == 4:
        first, second, last = (pick(table, me_s // 2) for table in DRAWS)
        across(first).start()
        across(second).start()
    else:
        each(1, chips, lambda d: across(chips - d).start())
    beside(0).start()

    spread = (
        lax.broadcasted_iota(jnp.int32, (comps, comps * 8), 1) >> 3
        == lax.broadcasted_iota(jnp.int32, (comps, comps * 8), 0)
    ).astype(f32).astype(bf16)
    turn = lax.broadcasted_iota(jnp.int32, (periods, comps * 8), 1) & 7
    loadings_copy.wait()
    rest = loadings[...]
    for i in range(3):
        term = rest.astype(bf16)
        rest = rest - term.astype(f32)
        wide = jnp.dot(term, spread, preferred_element_type=f32)
        full = jnp.concatenate([jnp.where(turn == r, wide, 0.0) for r in range(8)], axis=0)
        mix[i * periods * 8:(i + 1) * periods * 8, :] = full.astype(bf16)

    def pass_on(d):
        beside(d).wait_recv()
        beside(d).start()

    quarter = (lax.broadcasted_iota(jnp.int32, (n_site * 16, deep), 0) >> 2) & 3
    low = lax.broadcasted_iota(jnp.int32, (chips, 8, LANES), 1) < 4

    def product(t, k):
        x = drawn[:, 16 * k:16 * (k + 1), :].reshape(n_site * 16, deep).astype(f32)
        lhs = jnp.concatenate(
            [jnp.where(quarter == q, x, 0.0).astype(bf16) for q in range(QUARTERS)], axis=1
        )
        y = jnp.dot(lhs, weights[t, k], preferred_element_type=f32)
        y = y.reshape(n_site, 2, 8, LANES)
        y = y[:, 0] + y[:, 1]
        y = y + pltpu.roll(y, 4, 1)
        y = y.reshape(chips, 2, 8, LANES)
        return jnp.where(low, y[:, 0], y[:, 1])

    def f_copy(t, d):
        peer = me_c ^ d
        at = pl.ds(pl.multiple_of(me_c * ks * 8, 16), ks * 8)
        return pltpu.make_async_remote_copy(
            src_ref=sent_f.at[t, peer], dst_ref=got_f.at[t, :, at, :],
            send_sem=f_send.at[t, d], recv_sem=f_recv.at[t, d],
            device_id={"comp": peer}, device_id_type=MESH,
        )

    def fields(j, t):
        both = jnp.concatenate([product(t, 2 * j), product(t, 2 * j + 1)], axis=1).astype(bf16)
        sent_f[t, :, :, 16 * j:16 * (j + 1), :] = both.reshape(n_comp, groups, 16, LANES)

    def push_fields(t, tables):
        for table in tables:
            f_copy(t, pick(table, me_c)).start()

    def send_fields(t):
        push_fields(t, FIELDS[:1])
        at = pl.ds(pl.multiple_of(me_c * ks * 8, 16), ks * 8)
        got_f[t, :, at, :] = sent_f[t, me_c]

    def m_copy(t, d):
        peer = me_s ^ d
        return pltpu.make_async_remote_copy(
            src_ref=sent_m.at[t, peer], dst_ref=got_m.at[t, me_s],
            send_sem=m_send.at[t, d], recv_sem=m_recv.at[t, d],
            device_id={"site": peer}, device_id_type=MESH,
        )

    def push(t, tables):
        for table in tables:
            d = pick(table, me_s // 2) * 2
            m_copy(t, d + me_s % 2).start()
            m_copy(t, d + 1 - me_s % 2).start()

    def push_rest(t):
        if chips == 4:
            push(t, MOTIONS[2:])
            m_copy(t, 1).start()

    def motions(t):
        for d in range(1, n_comp):
            f_copy(t, d).wait_recv()
        mean = mean_v[:, t * LANES:(t + 1) * LANES]
        dev = sigma_v[:, t * LANES:(t + 1) * LANES]
        n = periods * 8

        def one(g):
            e = jnp.dot(mix[...], got_f[t, g], preferred_element_type=f32)
            e = (e[2 * n:] + e[n:2 * n]) + e[:n]
            m = mean[None] + dev[None] * e.reshape(8, periods, LANES)
            m = jnp.concatenate([m[:, :, :LANES // 2], m[:, :, LANES // 2:]], axis=1)
            sent_m[t, pl.ds(8 * g, 8)] = m.astype(bf16)

        each(0, groups, one)
        if chips == 4:
            push(t, MOTIONS[:2])
        else:
            each(1, n_site, lambda d: m_copy(t, n_site - d).start())
        m_keep(t).start()

    def m_keep(t):
        return pltpu.make_async_copy(sent_m.at[t, me_s], got_m.at[t, me_s], keep_sem.at[t])

    if chips == 4:
        across(second).wait_send()
        across(last).start()
    for t in range(chunks):
        for k in range(ks):
            load_w(t, k).wait()
    each(1, chips, pass_on)
    each(0, chips, lambda d: from_beside(d).wait_recv())
    for t in range(chunks):
        for j in range(pairs):
            fields(j, t)
        send_fields(t)
        if t > 0:
            push_fields(t - 1, FIELDS[1:])
    push_fields(chunks - 1, FIELDS[1:])
    mean_copy.wait()
    sigma_copy.wait()
    for t in range(chunks):
        motions(t)
    for t in range(chunks):
        push_rest(t)

    if chips == 4:
        across(first).wait_send()
        across(last).wait_send()
    else:
        each(1, chips, lambda d: across(d).wait_send())
    each(0, chips, lambda d: beside(d).wait_send())
    for t in range(chunks):
        for d in range(1, n_comp):
            f_copy(t, d).wait_send()
    for t in range(chunks):
        m_keep(t).wait()
        each(1, n_site, lambda d: m_copy(t, d).wait_send())
    for t in range(chunks):
        each(1, n_site, lambda d: m_copy(t, d).wait_recv())


def arrange(blocks, out):
    chunks, slabs, rows, half = blocks.shape
    periods = rows // 2

    def one(s):
        for t in range(chunks):
            x = blocks[t, s].astype(jnp.float32)
            for h in range(2):
                at = pl.multiple_of((s * chunks + t) * 2 * half + h * half, half)
                out[0, :, pl.ds(at, half)] = x[h * periods:(h + 1) * periods].astype(out.dtype)

    each(0, slabs, one)


def body(n_comp, n_site, factors, normals, loadings, mean_ln, sigma):
    ks, rank, s_dev = factors.shape
    rows = normals.shape[1]
    periods, comps = loadings.shape
    groups = n_site // 2 // n_comp
    chunks = s_dev // LANES
    assert rows == 4 and n_comp == rows and n_site % (2 * n_comp) == 0
    assert n_site & (n_site - 1) == 0
    assert ks % 2 == 0 and periods % 8 == 0 and s_dev % LANES == 0
    bf16 = jnp.bfloat16
    dma = pltpu.SemaphoreType.DMA
    any_ = pl.BlockSpec(memory_space=pl.ANY)
    blocks = pl.pallas_call(
        functools.partial(kernel, n_comp, n_site),
        out_shape=pltpu.VMEM((chunks, n_site, 2 * periods, LANES // 2), bf16),
        in_specs=[any_] * 5,
        out_specs=any_,
        scratch_shapes=[
            pltpu.VMEM((chunks, ks, rank, LANES), bf16),
            pltpu.VMEM(normals.shape, bf16),
            pltpu.VMEM(loadings.shape, jnp.float32),
            pltpu.VMEM((n_site, ks * 16, rank // QUARTERS), bf16),
            pltpu.VMEM((periods, s_dev), jnp.float32),
            pltpu.VMEM((periods, s_dev), jnp.float32),
            pltpu.VMEM((3 * periods * 8, comps * 8), bf16),
            pltpu.VMEM((chunks, n_comp, groups, ks * 8, LANES), bf16),
            pltpu.VMEM((chunks, groups, comps * 8, LANES), bf16),
            pltpu.VMEM((chunks, n_site, 2 * periods, LANES // 2), bf16),
            dma((chunks, ks)), dma((4,)),
            dma((n_site // 2,)), dma((n_site // 2,)), dma((n_site,)),
            dma((chunks, n_comp)), dma((chunks, n_comp)),
            dma((chunks, n_site)), dma((chunks, n_site)), dma((chunks,)),
        ],
        compiler_params=pltpu.CompilerParams(
            collective_id=0, has_side_effects=True, vmem_limit_bytes=40 * 1024 * 1024
        ),
        cost_estimate=pl.CostEstimate(
            flops=2 * ks * rows * n_site * rank * s_dev,
            bytes_accessed=2 * ks * rank * s_dev, transcendentals=0,
        ),
    )(*(pltpu.with_memory_space_constraint(x, pltpu.HBM) for x in (factors, normals, loadings, mean_ln, sigma)))
    return pl.pallas_call(
        arrange,
        out_shape=jax.ShapeDtypeStruct((1, periods, n_site * s_dev), bf16),
        in_specs=[pl.BlockSpec(memory_space=pltpu.VMEM)],
        out_specs=pl.BlockSpec(memory_space=pltpu.VMEM),
        compiler_params=pltpu.CompilerParams(vmem_limit_bytes=40 * 1024 * 1024),
    )(pltpu.with_memory_space_constraint(blocks, pltpu.VMEM))


def solution(mesh):
    in_specs = (
        P("comp", None, "site"),
        P("comp", "site", None),
        P(),
        P(None, "site"),
        P(None, "site"),
    )
    out_specs = P(("comp", "site"), None, None)
    run = functools.partial(body, mesh.shape["comp"], mesh.shape["site"])
    return jax.shard_map(run, mesh=mesh, in_specs=in_specs, out_specs=out_specs, check_vma=False)
```

```python
import functools

import jax
import jax.numpy as jnp
from jax import lax
from jax.experimental import pallas as pl
from jax.experimental.pallas import tpu as pltpu
from jax.sharding import PartitionSpec as P

MESH = pl.DeviceIdType.MESH
QUARTERS = 4
LANES = 256
FIELDS = (231, 186, 93)
DRAWS = (155, 117, 238)
MOTIONS = (230, 155, 125)


def each(start, stop, step):
    if stop - start <= 8:
        for i in range(start, stop):
            step(i)
    else:
        lax.fori_loop(start, stop, lambda i, carry: (step(i), carry)[1], 0)


def kernel(
    n_comp, n_site,
    factors, normals_h, loadings_h, mean_ln, sigma, got_m,
    weights, normals, loadings, drawn, mean_v, sigma_v, mix, sent_f, got_f, sent_m,
    w_sem, in_sem, d_send, d_pass, d_recv, f_send, f_recv, m_send, m_recv, keep_sem,
):
    me_c, me_s = lax.axis_index("comp"), lax.axis_index("site")
    ks, rows, rank = normals.shape
    periods, comps = loadings.shape
    s_dev = factors.shape[2]
    chunks = s_dev // LANES
    groups = n_site // 2 // n_comp
    chips = n_site // 2
    deep = rank // QUARTERS
    f32, bf16 = jnp.float32, jnp.bfloat16

    def load_w(t, k):
        lanes = pl.ds(t * LANES, LANES)
        return pltpu.make_async_copy(
            factors.at[k, :, lanes], weights.at[t, k], w_sem.at[t, k]
        )

    mean_copy = pltpu.make_async_copy(mean_ln, mean_v, in_sem.at[0])
    sigma_copy = pltpu.make_async_copy(sigma, sigma_v, in_sem.at[1])
    normals_copy = pltpu.make_async_copy(normals_h, normals, in_sem.at[2])
    loadings_copy = pltpu.make_async_copy(loadings_h, loadings, in_sem.at[3])
    normals_copy.start()

    barrier = pltpu.get_barrier_semaphore()

    def greet_s(d):
        pl.semaphore_signal(
            barrier, inc=1, device_id={"site": me_s ^ d}, device_id_type=MESH
        )

    def greet_c(d):
        pl.semaphore_signal(
            barrier, inc=1, device_id={"comp": me_c ^ d}, device_id_type=MESH
        )

    each(1, n_site, lambda d: greet_s(n_site - d))
    each(1, n_comp, lambda d: greet_c(n_comp - d))

    normals_copy.wait()
    loadings_copy.start()
    for t in range(chunks):
        for k in range(ks):
            load_w(t, k).start()
    mean_copy.start()
    sigma_copy.start()

    for k in range(ks):
        x = normals[k].astype(f32)
        x = jnp.concatenate([x[:, q * deep:(q + 1) * deep] for q in range(QUARTERS)], axis=0)
        drawn[me_s, 16 * k:16 * (k + 1), :] = x.astype(bf16)

    pl.semaphore_wait(barrier, n_site - 1 + n_comp - 1)

    pairs = ks // 2

    def draws(slot, send_sem, peer):
        return pltpu.make_async_remote_copy(
            src_ref=drawn.at[slot], dst_ref=drawn.at[slot],
            send_sem=send_sem, recv_sem=d_recv.at[slot],
            device_id={"site": peer}, device_id_type=MESH,
        )

    def across(d):
        return draws(me_s, d_send.at[d], me_s ^ (2 * d))

    def beside(d):
        return draws(me_s ^ (2 * d), d_pass.at[d], me_s ^ 1)

    def from_beside(d):
        return draws(me_s ^ (2 * d) ^ 1, d_pass.at[d], me_s ^ 1)

    def pick(table, at):
        return table // lax.shift_left(1, at * 2) % 4

    if chips == 4:
        first, second, last = (pick(table, me_s // 2) for table in DRAWS)
        across(first).start()
        across(second).start()
    else:
        each(1, chips, lambda d: across(chips - d).start())
    beside(0).start()

    spread = (
        lax.broadcasted_iota(jnp.int32, (comps, comps * 8), 1) >> 3
        == lax.broadcasted_iota(jnp.int32, (comps, comps * 8), 0)
    ).astype(f32).astype(bf16)
    turn = lax.broadcasted_iota(jnp.int32, (periods, comps * 8), 1) & 7
    loadings_copy.wait()
    rest = loadings[...]
    for i in range(3):
        term = rest.astype(bf16)
        rest = rest - term.astype(f32)
        wide = jnp.dot(term, spread, preferred_element_type=f32)
        full = jnp.concatenate([jnp.where(turn == r, wide, 0.0) for r in range(8)], axis=0)
        mix[i * periods * 8:(i + 1) * periods * 8, :] = full.astype(bf16)

    def pass_on(d):
        beside(d).wait_recv()
        beside(d).start()

    quarter = (lax.broadcasted_iota(jnp.int32, (n_site * 16, deep), 0) >> 2) & 3
    low = lax.broadcasted_iota(jnp.int32, (chips, 8, LANES), 1) < 4

    def product(t, k):
        x = drawn[:, 16 * k:16 * (k + 1), :].reshape(n_site * 16, deep).astype(f32)
        lhs = jnp.concatenate(
            [jnp.where(quarter == q, x, 0.0).astype(bf16) for q in range(QUARTERS)], axis=1
        )
        y = jnp.dot(lhs, weights[t, k], preferred_element_type=f32)
        y = y.reshape(n_site, 2, 8, LANES)
        y = y[:, 0] + y[:, 1]
        y = y + pltpu.roll(y, 4, 1)
        y = y.reshape(chips, 2, 8, LANES)
        return jnp.where(low, y[:, 0], y[:, 1])

    def f_copy(t, d):
        peer = me_c ^ d
        at = pl.ds(pl.multiple_of(me_c * ks * 8, 16), ks * 8)
        return pltpu.make_async_remote_copy(
            src_ref=sent_f.at[t, peer], dst_ref=got_f.at[t, :, at, :],
            send_sem=f_send.at[t, d], recv_sem=f_recv.at[t, d],
            device_id={"comp": peer}, device_id_type=MESH,
        )

    def fields(j, t):
        both = jnp.concatenate([product(t, 2 * j), product(t, 2 * j + 1)], axis=1).astype(bf16)
        sent_f[t, :, :, 16 * j:16 * (j + 1), :] = both.reshape(n_comp, groups, 16, LANES)

    def push_fields(t, tables):
        for table in tables:
            f_copy(t, pick(table, me_c)).start()

    def send_fields(t):
        push_fields(t, FIELDS[:1])
        at = pl.ds(pl.multiple_of(me_c * ks * 8, 16), ks * 8)
        got_f[t, :, at, :] = sent_f[t, me_c]

    def m_copy(t, d):
        peer = me_s ^ d
        return pltpu.make_async_remote_copy(
            src_ref=sent_m.at[t, peer], dst_ref=got_m.at[t, me_s],
            send_sem=m_send.at[t, d], recv_sem=m_recv.at[t, d],
            device_id={"site": peer}, device_id_type=MESH,
        )

    def push(t, tables):
        for table in tables:
            d = pick(table, me_s // 2) * 2
            m_copy(t, d + me_s % 2).start()
            m_copy(t, d + 1 - me_s % 2).start()

    def push_rest(t):
        if chips == 4:
            push(t, MOTIONS[2:])
            m_copy(t, 1).start()

    def motions(t):
        for d in range(1, n_comp):
            f_copy(t, d).wait_recv()
        mean = mean_v[:, t * LANES:(t + 1) * LANES]
        dev = sigma_v[:, t * LANES:(t + 1) * LANES]
        n = periods * 8

        def one(g):
            e = jnp.dot(mix[...], got_f[t, g], preferred_element_type=f32)
            e = (e[2 * n:] + e[n:2 * n]) + e[:n]
            m = mean[None] + dev[None] * e.reshape(8, periods, LANES)
            m = jnp.concatenate([m[:, :, :LANES // 2], m[:, :, LANES // 2:]], axis=1)
            sent_m[t, pl.ds(8 * g, 8)] = m.astype(bf16)

        each(0, groups, one)
        if chips == 4:
            push(t, MOTIONS[:2])
        else:
            each(1, n_site, lambda d: m_copy(t, n_site - d).start())
        m_keep(t).start()

    def m_keep(t):
        return pltpu.make_async_copy(sent_m.at[t, me_s], got_m.at[t, me_s], keep_sem.at[t])

    if chips == 4:
        across(second).wait_send()
        across(last).start()
    for t in range(chunks):
        for k in range(ks):
            load_w(t, k).wait()
    each(1, chips, pass_on)
    each(0, chips, lambda d: from_beside(d).wait_recv())
    for t in range(chunks):
        for j in range(pairs):
            fields(j, t)
        send_fields(t)
        if t > 0:
            push_fields(t - 1, FIELDS[1:])
    push_fields(chunks - 1, FIELDS[1:])
    mean_copy.wait()
    sigma_copy.wait()
    for t in range(chunks):
        motions(t)
    for t in range(chunks):
        push_rest(t)

    if chips == 4:
        across(first).wait_send()
        across(last).wait_send()
    else:
        each(1, chips, lambda d: across(d).wait_send())
    each(0, chips, lambda d: beside(d).wait_send())
    for t in range(chunks):
        for d in range(1, n_comp):
            f_copy(t, d).wait_send()
    for t in range(chunks):
        m_keep(t).wait()
        each(1, n_site, lambda d: m_copy(t, d).wait_send())
    for t in range(chunks):
        each(1, n_site, lambda d: m_copy(t, d).wait_recv())


def arrange(blocks, out):
    chunks, slabs, rows, half = blocks.shape
    periods = rows // 2

    def one(s):
        for t in range(chunks):
            x = blocks[t, s].astype(jnp.float32)
            for h in range(2):
                at = pl.multiple_of((s * chunks + t) * 2 * half + h * half, half)
                out[0, :, pl.ds(at, half)] = x[h * periods:(h + 1) * periods].astype(out.dtype)

    each(0, slabs, one)


def body(n_comp, n_site, factors, normals, loadings, mean_ln, sigma):
    ks, rank, s_dev = factors.shape
    rows = normals.shape[1]
    periods, comps = loadings.shape
    groups = n_site // 2 // n_comp
    chunks = s_dev // LANES
    assert rows == 4 and n_comp == rows and n_site % (2 * n_comp) == 0
    assert n_site & (n_site - 1) == 0
    assert ks % 2 == 0 and periods % 8 == 0 and s_dev % LANES == 0
    bf16 = jnp.bfloat16
    dma = pltpu.SemaphoreType.DMA
    any_ = pl.BlockSpec(memory_space=pl.ANY)
    blocks = pl.pallas_call(
        functools.partial(kernel, n_comp, n_site),
        out_shape=pltpu.VMEM((chunks, n_site, 2 * periods, LANES // 2), bf16),
        in_specs=[any_] * 5,
        out_specs=any_,
        scratch_shapes=[
            pltpu.VMEM((chunks, ks, rank, LANES), bf16),
            pltpu.VMEM(normals.shape, bf16),
            pltpu.VMEM(loadings.shape, jnp.float32),
            pltpu.VMEM((n_site, ks * 16, rank // QUARTERS), bf16),
            pltpu.VMEM((periods, s_dev), jnp.float32),
            pltpu.VMEM((periods, s_dev), jnp.float32),
            pltpu.VMEM((3 * periods * 8, comps * 8), bf16),
            pltpu.VMEM((chunks, n_comp, groups, ks * 8, LANES), bf16),
            pltpu.VMEM((chunks, groups, comps * 8, LANES), bf16),
            pltpu.VMEM((chunks, n_site, 2 * periods, LANES // 2), bf16),
            dma((chunks, ks)), dma((4,)),
            dma((n_site // 2,)), dma((n_site // 2,)), dma((n_site,)),
            dma((chunks, n_comp)), dma((chunks, n_comp)),
            dma((chunks, n_site)), dma((chunks, n_site)), dma((chunks,)),
        ],
        compiler_params=pltpu.CompilerParams(
            collective_id=0, has_side_effects=True, vmem_limit_bytes=40 * 1024 * 1024
        ),
        cost_estimate=pl.CostEstimate(
            flops=2 * ks * rows * n_site * rank * s_dev,
            bytes_accessed=2 * ks * rank * s_dev, transcendentals=0,
        ),
    )(*(pltpu.with_memory_space_constraint(x, pltpu.HBM) for x in (factors, normals, loadings, mean_ln, sigma)))
    return pl.pallas_call(
        arrange,
        out_shape=jax.ShapeDtypeStruct((1, periods, n_site * s_dev), bf16),
        in_specs=[pl.BlockSpec(memory_space=pltpu.VMEM)],
        out_specs=pl.BlockSpec(memory_space=pltpu.VMEM),
        compiler_params=pltpu.CompilerParams(vmem_limit_bytes=40 * 1024 * 1024),
    )(pltpu.with_memory_space_constraint(blocks, pltpu.VMEM))


def solution(mesh):
    in_specs = (
        P("comp", None, "site"),
        P("comp", "site", None),
        P(),
        P(None, "site"),
        P(None, "site"),
    )
    out_specs = P(("comp", "site"), None, None)
    run = functools.partial(body, mesh.shape["comp"], mesh.shape["site"])
    return jax.shard_map(run, mesh=mesh, in_specs=in_specs, out_specs=out_specs, check_vma=False)
```
